256 devices in a mesh: dp: 64 (over z, y, x_hi), tensor: 4 (over x_lo, core).
Axes of the slice: x: 4 (x_hi: 2, x_lo: 2; x = x_hi * 2 + x_lo), y: 4, z: 8, core: 2. Of those that a mesh axis runs over, the one named last changes fastest.
Arguments:
- queries: bfloat16 [2, 4096, 4096], P(None, 'dp', 'tensor'), may hold values from -14 to 14
- cached_key_rows: bfloat16 [4096, 192, 1024], P('dp', None, 'tensor'), may hold values from -6 to 6
- cached_value_rows: bfloat16 [4096, 192, 1024], P('dp', None, 'tensor'), may hold values from -6 to 6
- incoming_keys: bfloat16 [2, 4096, 1024], P(None, 'dp', 'tensor'), may hold values from -6 to 6
- incoming_values: bfloat16 [2, 4096, 1024], P(None, 'dp', 'tensor'), may hold values from -6 to 6
- output_weight: bfloat16 [4096, 4096], P('tensor'), may hold values from -0.125 to 0.125
- adapter_down_weight: bfloat16 [64, 4096, 256], P('dp', 'tensor'), may hold values from -0.09375 to 0.09375
- adapter_up_weight: bfloat16 [64, 256, 4096], P('dp', None, 'tensor'), may hold values from -0.375 to 0.375
- opponent: int32 [4096, 1], P('dp'), may hold values from 0 to 63; in each aligned block of 64 rows (0 to 63, 64 to 127, ...) at most 2 rows name the same one
- cache_length_rows: int32 [4096], P('dp'), may hold values from 1 to 192
Outputs:
- mixed: bfloat16 [2, 4096, 4096], P(None, 'dp', 'tensor')
The draws below stay inside these ranges and needn't reach their ends.
Inputs may be any that keep to these rules, and one draw needn't show every extreme that they name: In the 64 rows of one index of dp no opponent appears more than 2 times.
All inputs are finite; a program needn't handle non-finite values.
Results may differ from the reference program's by a relative error of at most 0.0061.
Values may be sent and summed in bfloat16 or wider, within the bound.
A program may use at most 192 MiB of HBM per device.

```python
import math
import jax
import jax.numpy as jnp
import numpy as np
from jax import lax

HEAD_SIZE = 128
QUERY_HEADS = 32
KEY_VALUE_HEADS = 8
OUTPUT_WIDTH = 4096
ADAPTER_RANK = 256
STEPS = 2
ROWS_DEV = 64
CONTEXT_LENGTH = 192
QUERY_WIDTH = 4096
KVDIM = 1024
ROWS = 4096
ADAPTER_COUNT = 64
CAP = 2
N_DP = 64


def draw_queries(key, part):
    key = jax.random.fold_in(key, 1)
    first = jax.random.fold_in(key, 0)
    value_rows = jnp.clip(jax.random.normal(first, (STEPS, ROWS, QUERY_WIDTH), jnp.float32), -6.0, 6.0)
    return value_rows.astype(jnp.bfloat16)


def draw_cached_key_rows(key, part):
    key = jax.random.fold_in(key, 2)
    first = jax.random.fold_in(key, 0)
    value_rows = jnp.clip(jax.random.normal(first, (ROWS, CONTEXT_LENGTH, KVDIM), jnp.float32), -6.0, 6.0)
    return value_rows.astype(jnp.bfloat16)


def draw_cache_length_rows(key, part):
    key = jax.random.fold_in(key, 3)
    first, second = jax.random.split(key, 2)
    lengths = jax.random.randint(first, (ROWS,), 1, CONTEXT_LENGTH + 1, dtype=jnp.int32)
    blocks = ROWS // ROWS_DEV
    picked_adapters = jax.random.randint(second, (blocks,), 0, ROWS_DEV, dtype=jnp.int32)
    positions = jnp.arange(blocks, dtype=jnp.int32) * ROWS_DEV + picked_adapters
    return lengths.at[positions].set(CONTEXT_LENGTH)


def raised(drawn, own_key, source, target, blocks, factor):
    def block_of(dim):
        return (jnp.arange(drawn.shape[dim]) // (drawn.shape[dim] // blocks)).reshape((-1,) + (1,) * (drawn.ndim - 1 - dim))

    near = jax.random.permutation(own_key, blocks)[block_of(target)]
    other_side = (block_of(target) + blocks // 2) % blocks
    return jnp.where((block_of(source) == near) | (block_of(source) == other_side), factor * drawn, drawn)


def steps_of(key, extent, cuts, smallest, top_value):
    def one(dim, shards_of):
        heights = jax.random.uniform(jax.random.fold_in(jax.random.fold_in(key, 6), dim), (shards_of,), jnp.float32, smallest / len(cuts), top_value / len(cuts))
        return jnp.repeat(jnp.exp(heights), extent[dim] // shards_of).reshape((-1,) + (1,) * (len(extent) - dim - 1))

    factor_of = one(*cuts[0])
    for cut in cuts[1:]:
        factor_of = factor_of * one(*cut)
    return factor_of


def shared_out(rng, own, number, rows, count, top, reach, lean):
    sequence = jax.random.permutation(rng, count)
    crowded, usual = portions_of(count, rows * top, reach, lean, True), portions_of(count, rows * top, reach, lean, False)
    places = jnp.arange(count)

    def named(tallies, offset_by):
        used = int((tallies > 0).sum())
        fixed = max(1, used // 4)
        passed = fixed + (places - fixed + offset_by * (used - fixed)) % max(1, count - fixed)
        return jnp.zeros((count,), jnp.int32).at[sequence[jnp.where(places < fixed, places, passed)]].set(jnp.asarray(tallies, jnp.int32))

    tallies = jnp.where(number % 4 == 0, named(crowded, number // 4), named(usual, number - number // 4 - 1))
    mixed = jax.random.permutation(jax.random.fold_in(own, 3), count)
    giver, sink = mixed[0:count // 2 * 2:2], mixed[1:count // 2 * 2:2]
    margin = jnp.minimum(tallies[giver] - 1, reach - tallies[sink]) // 2
    margin = jnp.where((giver == sequence[0]) | (sink == sequence[0]) | (tallies[sink] == 0), 0, jnp.maximum(margin, 0))
    passed = jax.random.randint(jax.random.fold_in(own, 4), (count // 2,), 0, 1 << 20) % (margin + 1)
    tallies = tallies.at[giver].add(-passed).at[sink].add(passed)
    members = jnp.searchsorted(jnp.cumsum(tallies), jnp.arange(rows * top), side="right").astype(jnp.int32)
    table = members.reshape(top, rows).T
    table = table[jax.random.permutation(jax.random.fold_in(own, 1), rows)]
    offset_by = jax.random.randint(jax.random.fold_in(own, 2), (rows, 1), 0, top)
    return jnp.take_along_axis(table, (jnp.arange(top)[None, :] + offset_by) % top, axis=1)


def portions_of(count, total, reach, lean, full):
    weights = [(1 << 20) // math.isqrt(grade ** lean) + 1 for grade in range(1, count + 1)]
    largest = reach if full else min(reach, max(-(-total // count), total * weights[0] // sum(weights)))
    least = 1 if total - largest >= count - 1 else 0
    given, surplus = [largest] + [least] * (count - 1), total - largest - least * (count - 1)
    while surplus > 0:
        movable = [i for i in range(1, count) if given[i] < largest] or [i for i in range(1, count) if given[i] < reach]
        mass, left = sum([weights[i] for i in movable]), surplus
        for i in movable:
            extra = min(reach - given[i], max(1, left * weights[i] // mass), surplus)
            given[i] = given[i] + extra
            surplus = surplus - extra
    return np.array(given)


def noise(stream_key, extent, scale, reach, pieces=(), kind=jnp.bfloat16):
    loudness = steps_of(stream_key, extent, pieces, -0.22, 0.18) if pieces else 1.0
    drawn = jax.random.normal(stream_key, extent, jnp.float32) * scale * loudness
    return jnp.minimum(jnp.maximum(drawn, -reach), reach).astype(kind)


def noise_with(key, shape, width, reach, pieces, heavy, kind=jnp.bfloat16):
    entries = width * jax.random.normal(key, shape, jnp.float32)
    if pieces:
        entries = entries * steps_of(key, shape, pieces, -0.22, 0.18)
    return jnp.clip(raised(entries, jax.random.fold_in(key, 3), *heavy), -reach, reach).astype(kind)


def setup_inputs(seed: int = 0) -> dict:
    key_list = jax.random.split(jax.random.key(seed), 11)
    queries = draw_queries(jax.random.fold_in(key_list[10], 71), 0)
    cached_key_rows = draw_cached_key_rows(jax.random.fold_in(key_list[10], 71), 0)
    cached_value_rows = noise(key_list[2], (ROWS, CONTEXT_LENGTH, KVDIM), 1.0, 6.0, ((0, 64), (2, 4)))
    incoming_keys = noise(key_list[3], (STEPS, ROWS, KVDIM), 1.0, 6.0, ((1, 64), (2, 4)))
    incoming_values = noise(key_list[4], (STEPS, ROWS, KVDIM), 1.0, 6.0, ((1, 64), (2, 4)))
    output_weight = noise_with(key_list[5], (QUERY_WIDTH, OUTPUT_WIDTH), QUERY_WIDTH ** -0.5, 0.125, ((0, 4),), (0, 1, 4, 2.0))
    adapter_down_weight = noise(key_list[6], (ADAPTER_COUNT, QUERY_WIDTH, ADAPTER_RANK), QUERY_WIDTH ** -0.5, 0.09375, ((0, 64), (1, 4)))
    adapter_up_weight = noise(key_list[7], (ADAPTER_COUNT, ADAPTER_RANK, OUTPUT_WIDTH), ADAPTER_RANK ** -0.5, 0.375, ((0, 64), (2, 4)))
    opponent_keys = jax.random.split(jax.random.fold_in(key_list[8], 1), ROWS // ROWS_DEV)
    opponent_turns = jax.random.permutation(jax.random.fold_in(key_list[8], 3), ROWS // ROWS_DEV)
    opponent = jax.vmap(lambda own, number: shared_out(jax.random.fold_in(key_list[8], 2), own, number, ROWS_DEV, ADAPTER_COUNT, 1, CAP, 2))(opponent_keys, opponent_turns).reshape((ROWS, 1))
    cache_length_rows = draw_cache_length_rows(jax.random.fold_in(key_list[10], 71), 0)
    return dict(queries=queries, cached_key_rows=cached_key_rows, cached_value_rows=cached_value_rows, incoming_keys=incoming_keys, incoming_values=incoming_values, output_weight=output_weight, adapter_down_weight=adapter_down_weight, adapter_up_weight=adapter_up_weight, opponent=opponent, cache_length_rows=cache_length_rows)


def attend_rows(query_vector, key_rows, value_rows, step_key_rows, step_value_rows, lengths):
    batch_row_count = query_vector.shape[0]
    group_count = QUERY_HEADS // KEY_VALUE_HEADS
    taken_weight = step_key_rows.shape[0]
    query_head_rows = query_vector.astype(jnp.float32).reshape(batch_row_count, KEY_VALUE_HEADS, group_count, HEAD_SIZE)
    key_head_rows = key_rows.astype(jnp.float32).reshape(batch_row_count, CONTEXT_LENGTH, KEY_VALUE_HEADS, HEAD_SIZE)
    value_head_rows = value_rows.astype(jnp.float32).reshape(batch_row_count, CONTEXT_LENGTH, KEY_VALUE_HEADS, HEAD_SIZE)
    step_key = step_key_rows.astype(jnp.float32).reshape(taken_weight, batch_row_count, KEY_VALUE_HEADS, HEAD_SIZE)
    step_value = step_value_rows.astype(jnp.float32).reshape(taken_weight, batch_row_count, KEY_VALUE_HEADS, HEAD_SIZE)
    scale = 1.0 / math.sqrt(HEAD_SIZE)
    cache_scores = jnp.einsum('rkgd,rpkd->rkgp', query_head_rows, key_head_rows) * scale
    live_mask = jnp.arange(CONTEXT_LENGTH)[None, :] < lengths[:, None]
    cache_scores = jnp.where(live_mask[:, None, None, :], cache_scores, -1e+30)
    fresh_scores = jnp.einsum('rkgd,trkd->rkgt', query_head_rows, step_key) * scale
    scores = jnp.concatenate([cache_scores, fresh_scores], axis=3)
    highest = lax.optimization_barrier(jnp.max(scores, axis=3, keepdims=True))
    powers = jnp.exp(scores - highest)
    probs = (powers / lax.optimization_barrier(jnp.sum(powers, axis=3, keepdims=True))).astype(jnp.bfloat16).astype(jnp.float32)
    result = jnp.einsum('rkgp,rpkd->rkgd', probs[..., :CONTEXT_LENGTH], value_head_rows)
    result = result + jnp.einsum('rkgt,trkd->rkgd', probs[..., CONTEXT_LENGTH:], step_value)
    return result.reshape(batch_row_count, QUERY_WIDTH).astype(jnp.bfloat16)

def reference(queries, cached_key_rows, cached_value_rows, incoming_keys, incoming_values, output_weight, adapter_down_weight, adapter_up_weight, opponent, cache_length_rows):
    blocks = ROWS // ROWS_DEV
    outputs = []
    for decode_step_index in range(STEPS):
        taken_weight = decode_step_index + 1
        query_blocks = queries[decode_step_index].reshape(blocks, ROWS_DEV, QUERY_WIDTH)
        key_blocks = cached_key_rows.reshape(blocks, ROWS_DEV, CONTEXT_LENGTH, KVDIM)
        value_blocks = cached_value_rows.reshape(blocks, ROWS_DEV, CONTEXT_LENGTH, KVDIM)
        step_key = incoming_keys[:taken_weight].reshape(taken_weight, blocks, ROWS_DEV, KVDIM).transpose(1, 0, 2, 3)
        step_value = incoming_values[:taken_weight].reshape(taken_weight, blocks, ROWS_DEV, KVDIM).transpose(1, 0, 2, 3)
        length_blocks = cache_length_rows.reshape(blocks, ROWS_DEV)

        def one_block(packed):
            return attend_rows(*packed)
        attended_output = lax.map(one_block, (query_blocks, key_blocks, value_blocks, step_key, step_value, length_blocks))
        outputs.append(attended_output.reshape(ROWS, QUERY_WIDTH))
    flattened = jnp.concatenate(outputs, axis=0)
    base = jnp.dot(flattened, output_weight, preferred_element_type=jnp.float32)
    opponent_rows = jnp.tile(opponent[:, 0], STEPS)
    capacity_rows = STEPS * N_DP * CAP

    def per_adapter(running, adapter_index):
        chosen = opponent_rows == adapter_index
        count = jnp.sum(chosen.astype(jnp.int32))
        index_list = jnp.nonzero(chosen, size=capacity_rows, fill_value=0)[0].astype(jnp.int32)
        valid = jnp.arange(capacity_rows) < count
        picked_adapters = flattened[index_list]
        shrunk_rows = jnp.dot(picked_adapters, adapter_down_weight[adapter_index], preferred_element_type=jnp.float32).astype(jnp.bfloat16)
        lifted_rows = jnp.dot(shrunk_rows, adapter_up_weight[adapter_index], preferred_element_type=jnp.float32).astype(jnp.bfloat16).astype(jnp.float32)
        return (running.at[index_list].add(jnp.where(valid[:, None], lifted_rows, jnp.float32(0.0))), None)
    lift, unused = lax.scan(per_adapter, jnp.zeros((STEPS * ROWS, OUTPUT_WIDTH), jnp.float32), jnp.arange(ADAPTER_COUNT, dtype=jnp.int32))
    mixed = (base + lift).astype(jnp.bfloat16)
    return mixed.reshape(STEPS, ROWS, OUTPUT_WIDTH)
```

```python
import math

import jax
import jax.numpy as jnp
from jax import lax
from jax.experimental import pallas as pl
from jax.experimental.pallas import tpu as pltpu
from jax.sharding import PartitionSpec as P

ROWS = 64
CACHE = 192
EXTENDED = 208
GROUP = 16
HEAD = 128
SCALE = 1.0 / math.sqrt(HEAD)
MESH = pl.DeviceIdType.MESH
CONTRACT_LAST = (((1,), (1,)), ((), ()))


def kernel(
    q_hbm, k_hbm, v_hbm, nk_hbm, nv_hbm, wo_hbm, wd_hbm, wu_hbm, len_ref, place_row, place_col,
    out_ref,
    qv, nkv, nvv, kb, vb, fresh, qs, att, attp, outward, homeward, wo, wd, wu,
    send, recv, recvf, part, x1r, x2s, x2r, shrunk, liftf, rsend, rrecv,
    attb, bsend, brecv, keep, csend, crecv,
    small_sem, kv_sem, w_sem, d_send, d_recv, r_send, r_recv, t_send, t_recv,
):
    dp = lax.axis_index("dp")
    t = lax.axis_index("tensor")
    z, y, xh = dp // 8, lax.rem(dp // 2, 4), lax.rem(dp, 2)
    core = lax.rem(t, 2)
    near = t + 1 - 2 * core
    far = lax.rem(t + 2, 4)
    near_far = lax.rem(near + 2, 4)

    def peer(j):
        k = j + (j + 57) // 64
        a, b = lax.rem(k, 8), k // 8
        dz = lax.rem(12 + ((a + 1) // 2) * (1 - 2 * lax.rem(a, 2)), 8)
        return lax.rem(z + dz, 8) * 8 + lax.rem(y + b // 2, 4) * 2 + lax.rem(xh + lax.rem(b, 2), 2)

    small = [
        pltpu.make_async_copy(a, b, small_sem.at[i])
        for i, (a, b) in enumerate(((q_hbm, qv), (nk_hbm, nkv), (nv_hbm, nvv)))
    ]
    for c in small:
        c.start()

    def kv_copies(g):
        rows = pl.ds(g * GROUP, GROUP)
        return (
            pltpu.make_async_copy(k_hbm.at[rows], kb.at[rows, pl.ds(0, CACHE)], kv_sem.at[0, g]),
            pltpu.make_async_copy(v_hbm.at[rows], vb.at[rows, pl.ds(0, CACHE)], kv_sem.at[1, g]),
        )

    for g in range(ROWS // GROUP):
        for c in kv_copies(g):
            c.start()
    weights = [
        pltpu.make_async_copy(
            wo_hbm.at[:, pl.ds(pl.multiple_of(block * 1024, 1024), 1024)], wo.at[i], w_sem.at[i]
        )
        for i, block in enumerate((near, near_far, far, t))
    ]
    weights.append(pltpu.make_async_copy(wd_hbm.at[0], wd, w_sem.at[4]))
    weights.append(pltpu.make_async_copy(wu_hbm.at[0], wu, w_sem.at[5]))
    for c in weights:
        c.start()

    barrier = pltpu.get_barrier_semaphore()

    def greet(j, carry):
        pl.semaphore_signal(barrier, inc=1, device_id=(peer(j), t), device_id_type=MESH)
        return carry

    lax.fori_loop(0, 63, greet, 0)
    for other in (near, far, near_far):
        pl.semaphore_signal(barrier, inc=1, device_id=(dp, other), device_id_type=MESH)

    for c in small:
        c.wait()
    for h in range(2):
        for s in range(2):
            for g in range(4):
                col = (h * 4 + g) * HEAD
                qs[h, pl.ds(s * 4 + g, ROWS, stride=8), :] = qv[s, :, col : col + HEAD].astype(jnp.float32)
    fresh[...] = jnp.zeros_like(fresh)
    for src, dst in ((nkv, kb), (nvv, vb)):
        for s in range(2):
            for h in range(2):
                fresh[h, pl.ds(s, ROWS, stride=16), :] = src[s, :, h * HEAD : (h + 1) * HEAD].astype(jnp.float32)
        for h in range(2):
            dst[:, CACHE:EXTENDED, h * HEAD : (h + 1) * HEAD] = (
                fresh[h].reshape(ROWS, 16, HEAD).astype(jnp.bfloat16)
            )

    def map_out(i, carry):
        rows = pl.ds(pl.multiple_of(i * 64, 64), 64)
        at = lax.broadcasted_iota(jnp.int32, (64, ROWS * 8), 0) + i * 64
        outward[rows, :] = jnp.where(at == place_row[...], 1.0, 0.0).astype(jnp.bfloat16)
        return carry

    lax.fori_loop(0, 16, map_out, 0)

    def map_home(i, carry):
        rows = pl.ds(pl.multiple_of(i * 32, 32), 32)
        at = lax.broadcasted_iota(jnp.int32, (32, ROWS * 16), 1)
        homeward[rows, :] = jnp.where(at == place_col[rows, :], 1.0, 0.0).astype(jnp.bfloat16)
        return carry

    lax.fori_loop(0, 16, map_home, 0)

    lane = lax.broadcasted_iota(jnp.int32, (8, EXTENDED), 1)
    sub = lax.broadcasted_iota(jnp.int32, (8, EXTENDED), 0)
    new_ok = (lane == CACHE) | ((lane == CACHE + 1) & (sub >= 4))
    zero = jnp.zeros((8, HEAD), jnp.float32)

    def probs(scores, r):
        ok = (lane < len_ref[r]) | new_ok
        scores = jnp.where(ok, scores * SCALE, -1e30)
        power = jnp.exp(scores - jnp.max(scores, axis=1, keepdims=True))
        return power / jnp.sum(power, axis=1, keepdims=True)

    def attend(g, carry):
        for c in kv_copies(g):
            c.wait()
        rows = [g * GROUP + j for j in range(GROUP)]
        at = [pl.ds(pl.multiple_of(r * 8, 8), 8) for r in rows]
        scores = []
        for r, a in zip(rows, at):
            q = jnp.concatenate(
                [jnp.concatenate([qs[0, a, :], zero], 1), jnp.concatenate([zero, qs[1, a, :]], 1)], 0
            ).astype(jnp.bfloat16)
            scores.append(lax.dot_general(q, kb[r], CONTRACT_LAST, preferred_element_type=jnp.float32))
        ps = [
            jnp.concatenate([probs(s[:8], r), probs(s[8:], r)], 0).astype(jnp.bfloat16)
            for s, r in zip(scores, rows)
        ]
        both = []
        for p, r, a in zip(ps, rows, at):
            o = jnp.dot(p, vb[r], preferred_element_type=jnp.float32)
            att[0, a, :] = o[:8, :HEAD]
            att[1, a, :] = o[8:, HEAD:]
            both.append(jnp.concatenate([o[:8, :HEAD], o[8:, HEAD:]], 1))
        for i in range(GROUP // 2):
            pair = pl.ds(pl.multiple_of(g * GROUP * 8 + i * 16, 16), 16)
            attp[pair, :] = jnp.concatenate(both[2 * i : 2 * i + 2], 0).astype(jnp.bfloat16)
        return carry

    lax.fori_loop(0, ROWS // GROUP, attend, 0)

    pl.semaphore_wait(barrier, 66)

    def fill(i, carry):
        rows = pl.ds(pl.multiple_of(i * 256, 256), 256)
        filled = jnp.dot(outward[rows, :], attp[...], preferred_element_type=jnp.float32)
        send[pl.ds(pl.multiple_of(i * 16, 16), 16)] = filled.astype(jnp.bfloat16).reshape(16, 16, 256)
        return carry

    lax.fori_loop(0, 4, fill, 0)

    def dispatch(i, carry):
        for j in range(7):
            d = peer(i * 7 + j)
            pltpu.make_async_remote_copy(
                src_ref=send.at[d], dst_ref=recv.at[dp], send_sem=d_send, recv_sem=d_recv,
                device_id=(d, t), device_id_type=MESH,
            ).start()
        return carry

    lax.fori_loop(0, 9, dispatch, 0)
    recv[dp] = send[dp]

    for h in range(2):
        for s in range(2):
            for g in range(4):
                col = (h * 4 + g) * HEAD
                attb[s * ROWS : (s + 1) * ROWS, col : col + HEAD] = att[
                    h, pl.ds(s * 4 + g, ROWS, stride=8), :
                ].astype(jnp.bfloat16)

    def base_block(i, store):
        weights[i].wait()

        def tile(n, carry):
            cols = pl.ds(pl.multiple_of(n * 256, 256), 256)
            store(cols, jnp.dot(attb[...], wo[i, :, cols], preferred_element_type=jnp.float32))
            return carry

        lax.fori_loop(0, 4, tile, 0)

    def remote(i, src, dst, other):
        return pltpu.make_async_remote_copy(
            src_ref=src, dst_ref=dst, send_sem=t_send.at[i], recv_sem=t_recv.at[i],
            device_id=(dp, other), device_id_type=MESH,
        )

    base_near = []
    for i in range(2):

        def to_send(cols, value, i=i):
            bsend[i, :, cols] = value.astype(jnp.bfloat16)

        base_block(i, to_send)
        c = remote(i, bsend.at[i], brecv.at[i], near)
        c.start()
        base_near.append(c)
    for i in range(2):

        def to_keep(cols, value, i=i):
            keep[i, :, cols] = value

        base_block(2 + i, to_keep)
    base_near[1].wait()
    csend[...] = (keep[0] + brecv[1].astype(jnp.float32)).astype(jnp.bfloat16)
    base_far = remote(2, csend, crecv, far)
    base_far.start()

    weights[4].wait()
    weights[5].wait()
    pltpu.make_async_copy(recv.at[pl.ds(0, 63)], recv.at[pl.ds(0, 63)], d_recv).wait()
    for h in range(2):
        recvf[h] = recv[:, :, h * HEAD : (h + 1) * HEAD].reshape(16 * ROWS, HEAD).astype(jnp.float32)
    received = jnp.concatenate(
        [recvf[h, pl.ds(g, 4 * ROWS, stride=4), :].astype(jnp.bfloat16) for h in range(2) for g in range(4)], 1
    )
    part[...] = jnp.dot(received, wd[...], preferred_element_type=jnp.float32)
    mine = pl.ds(pl.multiple_of(core * 128, 128), 128)
    theirs = pl.ds(pl.multiple_of((1 - core) * 128, 128), 128)
    x1 = remote(3, part.at[theirs], x1r, near)
    x1.start()
    x1.wait()
    pair_sum = part[mine, :] + x1r[...]
    x2s[...] = pair_sum.astype(jnp.bfloat16)
    x2 = remote(4, x2s, x2r, far)
    x2.start()
    x2.wait()
    shrunk[mine, :] = (part[mine, :] + x1r[...] + x2r[...].astype(jnp.float32)).astype(jnp.bfloat16)
    x3 = remote(5, shrunk.at[mine], shrunk.at[mine], near)
    x3.start()
    x3.wait()

    for c in range(4):
        lifted = jnp.dot(shrunk[...], wu[:, c * 256 : (c + 1) * 256], preferred_element_type=jnp.float32)
        for h in range(2):
            liftf[h, pl.ds(c, 4 * ROWS, stride=4), :] = lifted[:, h * HEAD : (h + 1) * HEAD]
    for h in range(2):
        rsend[:, :, h * HEAD : (h + 1) * HEAD] = liftf[h].reshape(ROWS, 16, HEAD).astype(jnp.bfloat16)
    rrecv[dp] = rsend[dp]

    def give_back(i, carry):
        for j in range(7):
            d = peer(i * 7 + j)
            pltpu.make_async_remote_copy(
                src_ref=rsend.at[d], dst_ref=rrecv.at[dp], send_sem=r_send, recv_sem=r_recv,
                device_id=(d, t), device_id_type=MESH,
            ).start()
        return carry

    lax.fori_loop(0, 9, give_back, 0)

    base_near[0].wait()
    base_far.wait()
    keep[1] = keep[1] + brecv[0].astype(jnp.float32) + crecv[...].astype(jnp.float32)
    pltpu.make_async_copy(rrecv.at[pl.ds(0, 63)], rrecv.at[pl.ds(0, 63)], r_recv).wait()

    for c in range(4):
        cols = slice(c * 256, (c + 1) * 256)
        lifts = jnp.dot(
            homeward[c * 128 : (c + 1) * 128, :], rrecv[...].reshape(ROWS * 16, 256), preferred_element_type=jnp.float32
        )
        for s in range(2):
            rows = slice(s * ROWS, (s + 1) * ROWS)
            out_ref[s, :, cols] = (keep[1, rows, cols] + lifts[rows]).astype(jnp.bfloat16)
    pltpu.make_async_copy(send.at[pl.ds(0, 63)], send.at[pl.ds(0, 63)], d_send).wait()
    pltpu.make_async_copy(rsend.at[pl.ds(0, 63)], rsend.at[pl.ds(0, 63)], r_send).wait()


def local(
    queries,
    cached_key_rows,
    cached_value_rows,
    incoming_keys,
    incoming_values,
    output_weight,
    adapter_down_weight,
    adapter_up_weight,
    opponent,
    cache_length_rows,
):
    ids = opponent[:, 0]
    place = jnp.arange(ROWS, dtype=jnp.int32)
    earlier = (ids[:, None] == ids[None, :]) & (place[None, :] < place[:, None])
    slot_of_row = 2 * ids + jnp.sum(earlier.astype(jnp.int32), axis=1)
    eight = jnp.arange(8, dtype=jnp.int32)
    place_row = (slot_of_row[:, None] * 8 + eight[None, :]).reshape(1, ROWS * 8)
    quarter, step = jnp.arange(4, dtype=jnp.int32), jnp.arange(2, dtype=jnp.int32)
    place_col = (
        slot_of_row[None, None, :] * 8 + step[None, :, None] * 4 + quarter[:, None, None]
    ).reshape(ROWS * 8, 1)
    bf16, f32 = jnp.bfloat16, jnp.float32
    vmem, dma = pltpu.VMEM, pltpu.SemaphoreType.DMA
    hbm = pl.BlockSpec(memory_space=pl.ANY)
    smem = pl.BlockSpec(memory_space=pltpu.SMEM)
    return pl.pallas_call(
        kernel,
        out_shape=jax.ShapeDtypeStruct((2, ROWS, 1024), bf16),
        in_specs=[hbm] * 8 + [smem] + [pl.BlockSpec(memory_space=pltpu.VMEM)] * 2,
        out_specs=pl.BlockSpec(memory_space=pltpu.VMEM),
        scratch_shapes=[
            vmem((2, ROWS, 1024), bf16),
            vmem((2, ROWS, 256), bf16),
            vmem((2, ROWS, 256), bf16),
            vmem((ROWS, EXTENDED, 256), bf16),
            vmem((ROWS, EXTENDED, 256), bf16),
            vmem((2, ROWS * 16, HEAD), f32),
            vmem((2, ROWS * 8, HEAD), f32),
            vmem((2, ROWS * 8, HEAD), f32),
            vmem((ROWS * 8, 256), bf16),
            vmem((ROWS * 16, ROWS * 8), bf16),
            vmem((ROWS * 8, ROWS * 16), bf16),
            vmem((4, 1024, 1024), bf16),
            vmem((1024, 256), bf16),
            vmem((256, 1024), bf16),
            vmem((ROWS, 16, 256), bf16),
            vmem((ROWS, 16, 256), bf16),
            vmem((2, ROWS * 16, HEAD), f32),
            vmem((256, 256), f32),
            vmem((128, 256), f32),
            vmem((128, 256), bf16),
            vmem((128, 256), bf16),
            vmem((256, 256), bf16),
            vmem((2, ROWS * 16, HEAD), f32),
            vmem((ROWS, 16, 256), bf16),
            vmem((ROWS, 16, 256), bf16),
            vmem((2 * ROWS, 1024), bf16),
            vmem((2, 2 * ROWS, 1024), bf16),
            vmem((2, 2 * ROWS, 1024), bf16),
            vmem((2, 2 * ROWS, 1024), f32),
            vmem((2 * ROWS, 1024), bf16),
            vmem((2 * ROWS, 1024), bf16),
            dma((3,)),
            dma((2, 4)),
            dma((6,)),
            dma,
            dma,
            dma,
            dma,
            dma((6,)),
            dma((6,)),
        ],
        compiler_params=pltpu.CompilerParams(
            collective_id=0, has_side_effects=True, vmem_limit_bytes=56 << 20
        ),
        cost_estimate=pl.CostEstimate(flops=1500000000, bytes_accessed=24000000, transcendentals=300000),
    )(
        queries,
        cached_key_rows,
        cached_value_rows,
        incoming_keys,
        incoming_values,
        output_weight,
        adapter_down_weight,
        adapter_up_weight,
        cache_length_rows,
        place_row,
        place_col,
    )


def solution(mesh):
    in_specs = (
        P(None, "dp", "tensor"),
        P("dp", None, "tensor"),
        P("dp", None, "tensor"),
        P(None, "dp", "tensor"),
        P(None, "dp", "tensor"),
        P("tensor", None),
        P("dp", "tensor", None),
        P("dp", None, "tensor"),
        P("dp", None),
        P("dp"),
    )
    out_specs = P(None, "dp", "tensor")
    return jax.shard_map(local, mesh=mesh, in_specs=in_specs, out_specs=out_specs, check_vma=False)
```

```python
import math

import jax
import jax.numpy as jnp
from jax import lax
from jax.experimental import pallas as pl
from jax.experimental.pallas import tpu as pltpu
from jax.sharding import PartitionSpec as P

ROWS = 64
CACHE = 192
EXTENDED = 208
GROUP = 16
HEAD = 128
SCALE = 1.0 / math.sqrt(HEAD)
MESH = pl.DeviceIdType.MESH
CONTRACT_LAST = (((1,), (1,)), ((), ()))


def kernel(
    q_hbm, k_hbm, v_hbm, nk_hbm, nv_hbm, wo_hbm, wd_hbm, wu_hbm, len_ref, opp_ref,
    out_ref,
    qv, nkv, nvv, kb, vb, fresh, qs, att, attp, place_row, place_col, outward, homeward, wo, wd, wu,
    send, recv, recvf, part, x1r, shrunk, liftf, rsend, rrecv,
    attb, bsend, brecv, keep, csend, crecv,
    small_sem, kv_sem, w_sem, d_send, d_recv, r_send, r_recv, t_send, t_recv,
):
    dp = lax.axis_index("dp")
    t = lax.axis_index("tensor")
    z, y, xh = dp // 8, lax.rem(dp // 2, 4), lax.rem(dp, 2)
    core = lax.rem(t, 2)
    near = t + 1 - 2 * core
    far = lax.rem(t + 2, 4)
    near_far = lax.rem(near + 2, 4)

    order = (4, 3, 5, 2, 6, 1, 7, 0)
    ahead = [lax.rem(z + dz, 8) * 8 for dz in order]
    behind = [lax.rem(z + 8 - dz, 8) * 8 for dz in order]

    def across(b, sign):
        c = b // 2
        dy = lax.rem(2 * c, 4) + c // 2
        return lax.rem(y + 4 + sign * dy, 4) * 2 + lax.rem(xh + lax.rem(b, 2), 2)

    def each(first, last, planes, sign, step):
        if first == 0:
            for a in range(7):
                step(a, planes[a] + across(0, sign))

        def body(b, carry):
            plane = across(b, sign)
            for a in range(8):
                step(b * 8 + a, planes[a] + plane)
            return carry

        lax.fori_loop(max(first, 1), last, body, 0)

    small = [
        pltpu.make_async_copy(a, b, small_sem.at[i])
        for i, (a, b) in enumerate(((q_hbm, qv), (nk_hbm, nkv), (nv_hbm, nvv)))
    ]
    for c in small:
        c.start()

    def kv_copies(g):
        rows = pl.ds(g * GROUP, GROUP)
        return (
            pltpu.make_async_copy(k_hbm.at[rows], kb.at[rows, pl.ds(0, CACHE)], kv_sem.at[0, g]),
            pltpu.make_async_copy(v_hbm.at[rows], vb.at[rows, pl.ds(0, CACHE)], kv_sem.at[1, g]),
        )

    for g in range(ROWS // GROUP):
        for c in kv_copies(g):
            c.start()
    weights = [
        pltpu.make_async_copy(
            wo_hbm.at[:, pl.ds(pl.multiple_of(block * 1024, 1024), 1024)], wo.at[i], w_sem.at[i]
        )
        for i, block in enumerate((near, near_far, far, t))
    ]
    weights.append(pltpu.make_async_copy(wd_hbm.at[0], wd, w_sem.at[4]))
    weights.append(pltpu.make_async_copy(wu_hbm.at[0], wu, w_sem.at[5]))
    barrier = pltpu.get_barrier_semaphore()

    def greet(k, d):
        pl.semaphore_signal(barrier, inc=1, device_id=(d, t), device_id_type=MESH)

    each(0, 8, ahead, 1, greet)
    for other in (near, far, near_far):
        pl.semaphore_signal(barrier, inc=1, device_id=(dp, other), device_id_type=MESH)

    for c in small:
        c.wait()
    for h in range(2):
        for s in range(2):
            for g in range(4):
                col = (h * 4 + g) * HEAD
                qs[h, pl.ds(s * 4 + g, ROWS, stride=8), :] = qv[s, :, col : col + HEAD].astype(jnp.float32)
    fresh[...] = jnp.zeros_like(fresh)
    for src, dst in ((nkv, kb), (nvv, vb)):
        for s in range(2):
            for h in range(2):
                fresh[h, pl.ds(s, ROWS, stride=16), :] = src[s, :, h * HEAD : (h + 1) * HEAD].astype(jnp.float32)
        for h in range(2):
            dst[:, CACHE:EXTENDED, h * HEAD : (h + 1) * HEAD] = (
                fresh[h].reshape(ROWS, 16, HEAD).astype(jnp.bfloat16)
            )

    ids = opp_ref[...]
    down = lax.broadcasted_iota(jnp.int32, (ROWS, ROWS), 0)
    along = lax.broadcasted_iota(jnp.int32, (ROWS, ROWS), 1)
    named = jnp.where(down == ids, 1.0, 0.0)
    before = jnp.where(down < along, 1.0, 0.0).astype(jnp.bfloat16)
    earlier = jnp.dot(named.astype(jnp.bfloat16), before, preferred_element_type=jnp.float32)
    rank = jnp.sum(named * earlier, axis=0, keepdims=True).astype(jnp.int32)
    slot = jnp.sum(jnp.where(down == along, 2 * ids + rank, 0), axis=1, keepdims=True)
    place_col[...] = jnp.broadcast_to(slot * 8, (ROWS, HEAD))
    lanes = lax.broadcasted_iota(jnp.int32, (ROWS, ROWS * 8), 1)
    rows_of = lax.broadcasted_iota(jnp.int32, (ROWS, ROWS * 8), 0)
    place_row[...] = jnp.sum(
        jnp.where((lanes >> 3) == rows_of, slot * 8 + (lanes & 7), 0), axis=0, keepdims=True
    )

    lane = lax.broadcasted_iota(jnp.int32, (8, EXTENDED), 1)
    sub = lax.broadcasted_iota(jnp.int32, (8, EXTENDED), 0)
    new_ok = (lane == CACHE) | ((lane == CACHE + 1) & (sub >= 4))
    zero = jnp.zeros((8, HEAD), jnp.float32)

    def probs(scores, r):
        ok = (lane < len_ref[r]) | new_ok
        scores = jnp.where(ok, scores * SCALE, -1e30)
        power = jnp.exp(scores - jnp.max(scores, axis=1, keepdims=True))
        return power / jnp.sum(power, axis=1, keepdims=True)

    def attend(g, carry):
        for c in kv_copies(g):
            c.wait()

        @pl.when(g == 2)
        def _():
            for c in weights:
                c.start()

        for j in range(4):
            first = g * 256 + j * 64
            at = lax.broadcasted_iota(jnp.int32, (64, ROWS * 8), 0) + first
            outward[pl.ds(pl.multiple_of(first, 64), 64), :] = jnp.where(
                at == place_row[...], 1.0, 0.0
            ).astype(jnp.bfloat16)
        rows = [g * GROUP + j for j in range(GROUP)]
        at = [pl.ds(pl.multiple_of(r * 8, 8), 8) for r in rows]
        scores = []
        for r, a in zip(rows, at):
            q = jnp.concatenate(
                [jnp.concatenate([qs[0, a, :], zero], 1), jnp.concatenate([zero, qs[1, a, :]], 1)], 0
            ).astype(jnp.bfloat16)
            scores.append(lax.dot_general(q, kb[r], CONTRACT_LAST, preferred_element_type=jnp.float32))
        ps = [
            jnp.concatenate([probs(s[:8], r), probs(s[8:], r)], 0).astype(jnp.bfloat16)
            for s, r in zip(scores, rows)
        ]
        both = []
        for p, r, a in zip(ps, rows, at):
            o = jnp.dot(p, vb[r], preferred_element_type=jnp.float32)
            att[0, a, :] = o[:8, :HEAD]
            att[1, a, :] = o[8:, HEAD:]
            both.append(jnp.concatenate([o[:8, :HEAD], o[8:, HEAD:]], 1))
        for i in range(GROUP // 2):
            pair = pl.ds(pl.multiple_of(g * GROUP * 8 + i * 16, 16), 16)
            attp[pair, :] = jnp.concatenate(both[2 * i : 2 * i + 2], 0).astype(jnp.bfloat16)
        return carry

    lax.fori_loop(0, ROWS // GROUP, attend, 0)

    pl.semaphore_wait(barrier, 66)

    def fill(i, carry):
        rows = pl.ds(pl.multiple_of(i * 256, 256), 256)
        filled = jnp.dot(outward[rows, :], attp[...], preferred_element_type=jnp.float32)
        send[pl.ds(pl.multiple_of(i * 16, 16), 16)] = filled.astype(jnp.bfloat16).reshape(16, 16, 256)
        return carry

    lax.fori_loop(0, 4, fill, 0)

    def dispatch(half):
        def step(k, d):
            pltpu.make_async_remote_copy(
                src_ref=send.at[d], dst_ref=recv.at[k], send_sem=d_send, recv_sem=d_recv.at[half],
                device_id=(d, t), device_id_type=MESH,
            ).start()

        each(4 * half, 4 * half + 4, ahead, 1, step)

    dispatch(0)
    recv[7] = send[dp]

    for h in range(2):
        for s in range(2):
            for g in range(4):
                col = (h * 4 + g) * HEAD
                attb[s * ROWS : (s + 1) * ROWS, col : col + HEAD] = att[
                    h, pl.ds(s * 4 + g, ROWS, stride=8), :
                ].astype(jnp.bfloat16)

    def base_block(i, store):
        weights[i].wait()

        def tile(n, carry):
            cols = pl.ds(pl.multiple_of(n * 256, 256), 256)
            store(cols, jnp.dot(attb[...], wo[i, :, cols], preferred_element_type=jnp.float32))
            return carry

        lax.fori_loop(0, 4, tile, 0)

    def remote(i, src, dst, other):
        return pltpu.make_async_remote_copy(
            src_ref=src, dst_ref=dst, send_sem=t_send.at[i], recv_sem=t_recv.at[i],
            device_id=(dp, other), device_id_type=MESH,
        )

    base_near = []
    for i in range(2):

        def to_send(cols, value, i=i):
            bsend[i, :, cols] = value.astype(jnp.bfloat16)

        base_block(i, to_send)
        c = remote(i, bsend.at[i], brecv.at[i], near)
        c.start()
        base_near.append(c)
    dispatch(1)
    for i in range(2):

        def to_keep(cols, value, i=i):
            keep[i, :, cols] = value

        base_block(2 + i, to_keep)

    lane = lax.broadcasted_iota(jnp.int32, (ROWS, HEAD), 1)
    for c in range(4):
        for s in range(2):
            for n in range(8):
                homeward[(c * 2 + s) * ROWS : (c * 2 + s + 1) * ROWS, n * HEAD : (n + 1) * HEAD] = jnp.where(
                    lane + (n * HEAD - s * 4 - c) == place_col[...], 1.0, 0.0
                ).astype(jnp.bfloat16)

    weights[4].wait()
    weights[5].wait()

    def give_back(k, d):
        pltpu.make_async_remote_copy(
            src_ref=rsend.at[k], dst_ref=rrecv.at[dp], send_sem=r_send, recv_sem=r_recv,
            device_id=(d, t), device_id_type=MESH,
        ).start()

    others = (near, far, near_far)
    mine = pl.ds(pl.multiple_of(t * 32, 32), 32)
    for half in range(2):
        blocks = slice(half * 32, half * 32 + 32)
        count = 31 + half
        arrived = recv.at[pl.ds(half * 32, count)]
        pltpu.make_async_copy(arrived, arrived, d_recv.at[half]).wait()
        for h in range(2):
            recvf[h] = recv[blocks, :, h * HEAD : (h + 1) * HEAD].reshape(8 * ROWS, HEAD).astype(jnp.float32)
        received = jnp.concatenate(
            [
                recvf[h, pl.ds(g, 2 * ROWS, stride=4), :].astype(jnp.bfloat16)
                for h in range(2)
                for g in range(4)
            ],
            1,
        )
        part[half] = jnp.dot(received, wd[...], preferred_element_type=jnp.float32)
        sums = []
        for i, other in enumerate(others):
            rows = pl.ds(pl.multiple_of(other * 32, 32), 32)
            c = remote(3 + half * 6 + i, part.at[half, rows], x1r.at[half, i], other)
            c.start()
            sums.append(c)
        for c in sums:
            c.wait()
        total = part[half, mine, :] + x1r[half, 0] + (x1r[half, 1] + x1r[half, 2])
        shrunk[half, mine, :] = total.astype(jnp.bfloat16)
        shares = []
        for i, other in enumerate(others):
            c = remote(6 + half * 6 + i, shrunk.at[half, mine], shrunk.at[half, mine], other)
            c.start()
            shares.append(c)
        for c in shares:
            c.wait()
        for c in range(4):
            lifted = jnp.dot(shrunk[half], wu[:, c * 256 : (c + 1) * 256], preferred_element_type=jnp.float32)
            for h in range(2):
                liftf[h, pl.ds(c, 2 * ROWS, stride=4), :] = lifted[:, h * HEAD : (h + 1) * HEAD]
        for h in range(2):
            rsend[blocks, :, h * HEAD : (h + 1) * HEAD] = (
                liftf[h].reshape(ROWS // 2, 16, HEAD).astype(jnp.bfloat16)
            )
        if half == 0:
            rrecv[dp] = rsend[7]
        each(4 * half, 4 * half + 4, behind, -1, give_back)

    base_near[1].wait()
    csend[...] = (keep[0] + brecv[1].astype(jnp.float32)).astype(jnp.bfloat16)
    base_far = remote(2, csend, crecv, far)
    base_far.start()
    base_near[0].wait()
    base_far.wait()
    keep[1] = keep[1] + brecv[0].astype(jnp.float32) + crecv[...].astype(jnp.float32)
    pltpu.make_async_copy(rrecv.at[pl.ds(0, 63)], rrecv.at[pl.ds(0, 63)], r_recv).wait()

    lifts = jnp.dot(homeward[...], rrecv[...].reshape(ROWS * 16, 256), preferred_element_type=jnp.float32)
    for c in range(4):
        for s in range(2):
            rows, first = slice(s * ROWS, (s + 1) * ROWS), (c * 2 + s) * ROWS
            cols = slice(c * 256, (c + 1) * 256)
            out_ref[s, :, cols] = (keep[1, rows, cols] + lifts[first : first + ROWS]).astype(jnp.bfloat16)
    pltpu.make_async_copy(send.at[pl.ds(0, 63)], send.at[pl.ds(0, 63)], d_send).wait()
    pltpu.make_async_copy(rsend.at[pl.ds(0, 63)], rsend.at[pl.ds(0, 63)], r_send).wait()


def local(
    queries,
    cached_key_rows,
    cached_value_rows,
    incoming_keys,
    incoming_values,
    output_weight,
    adapter_down_weight,
    adapter_up_weight,
    opponent,
    cache_length_rows,
):
    bf16, f32 = jnp.bfloat16, jnp.float32
    vmem, dma = pltpu.VMEM, pltpu.SemaphoreType.DMA
    hbm = pl.BlockSpec(memory_space=pl.ANY)
    smem = pl.BlockSpec(memory_space=pltpu.SMEM)
    return pl.pallas_call(
        kernel,
        out_shape=jax.ShapeDtypeStruct((2, ROWS, 1024), bf16),
        in_specs=[hbm] * 8 + [smem] + [pl.BlockSpec(memory_space=pltpu.VMEM)],
        out_specs=pl.BlockSpec(memory_space=pltpu.VMEM),
        scratch_shapes=[
            vmem((2, ROWS, 1024), bf16),
            vmem((2, ROWS, 256), bf16),
            vmem((2, ROWS, 256), bf16),
            vmem((ROWS, EXTENDED, 256), bf16),
            vmem((ROWS, EXTENDED, 256), bf16),
            vmem((2, ROWS * 16, HEAD), f32),
            vmem((2, ROWS * 8, HEAD), f32),
            vmem((2, ROWS * 8, HEAD), f32),
            vmem((ROWS * 8, 256), bf16),
            vmem((1, ROWS * 8), jnp.int32),
            vmem((ROWS, HEAD), jnp.int32),
            vmem((ROWS * 16, ROWS * 8), bf16),
            vmem((ROWS * 8, ROWS * 16), bf16),
            vmem((4, 1024, 1024), bf16),
            vmem((1024, 256), bf16),
            vmem((256, 1024), bf16),
            vmem((ROWS, 16, 256), bf16),
            vmem((ROWS, 16, 256), bf16),
            vmem((2, ROWS * 8, HEAD), f32),
            vmem((2, 128, 256), f32),
            vmem((2, 3, 32, 256), f32),
            vmem((2, 128, 256), bf16),
            vmem((2, ROWS * 8, HEAD), f32),
            vmem((ROWS, 16, 256), bf16),
            vmem((ROWS, 16, 256), bf16),
            vmem((2 * ROWS, 1024), bf16),
            vmem((2, 2 * ROWS, 1024), bf16),
            vmem((2, 2 * ROWS, 1024), bf16),
            vmem((2, 2 * ROWS, 1024), f32),
            vmem((2 * ROWS, 1024), bf16),
            vmem((2 * ROWS, 1024), bf16),
            dma((3,)),
            dma((2, 4)),
            dma((6,)),
            dma,
            dma((2,)),
            dma,
            dma,
            dma((15,)),
            dma((15,)),
        ],
        compiler_params=pltpu.CompilerParams(
            collective_id=0, has_side_effects=True, vmem_limit_bytes=56 << 20
        ),
        cost_estimate=pl.CostEstimate(flops=1500000000, bytes_accessed=24000000, transcendentals=300000),
    )(
        queries,
        cached_key_rows,
        cached_value_rows,
        incoming_keys,
        incoming_values,
        output_weight,
        adapter_down_weight,
        adapter_up_weight,
        cache_length_rows,
        opponent.reshape(1, ROWS),
    )


def solution(mesh):
    in_specs = (
        P(None, "dp", "tensor"),
        P("dp", None, "tensor"),
        P("dp", None, "tensor"),
        P(None, "dp", "tensor"),
        P(None, "dp", "tensor"),
        P("tensor", None),
        P("dp", "tensor", None),
        P("dp", None, "tensor"),
        P("dp", None),
        P("dp"),
    )
    out_specs = P(None, "dp", "tensor")
    return jax.shard_map(local, mesh=mesh, in_specs=in_specs, out_specs=out_specs, check_vma=False)
```

```python
import math

import jax
import jax.numpy as jnp
from jax import lax
from jax.experimental import pallas as pl
from jax.experimental.pallas import tpu as pltpu
from jax.sharding import PartitionSpec as P

ROWS = 64
CACHE = 192
EXTENDED = 208
GROUP = 16
HEAD = 128
SCALE = 1.0 / math.sqrt(HEAD)
MESH = pl.DeviceIdType.MESH
CONTRACT_LAST = (((1,), (1,)), ((), ()))


def kernel(
    q_hbm, k_hbm, v_hbm, nk_hbm, nv_hbm, wo_hbm, wd_hbm, wu_hbm, len_ref, opp_ref,
    out_ref,
    qv, nkv, nvv, kb, vb, fresh, qs, att, attp, place_row, place_col, outward, homeward, wo, wd, wu,
    send, recv, recvf, part, x1r, pair, x2r, shrunk, liftf, rsend, rrecv,
    attb, bsend, brecv, keep, csend, crecv,
    small_sem, kv_sem, w_sem, d_send, d_recv, r_send, r_recv, t_send, t_recv,
):
    dp = lax.axis_index("dp")
    t = lax.axis_index("tensor")
    z, y, xh = dp // 8, lax.rem(dp // 2, 4), lax.rem(dp, 2)
    core = lax.rem(t, 2)
    near = t + 1 - 2 * core
    far = lax.rem(t + 2, 4)
    near_far = lax.rem(near + 2, 4)

    order = (4, 3, 5, 2, 6, 1, 7, 0)
    ahead = [lax.rem(z + dz, 8) * 8 for dz in order]
    behind = [lax.rem(z + 8 - dz, 8) * 8 for dz in order]

    def across(b, sign):
        c = b // 2
        dy = lax.rem(2 * c, 4) + c // 2
        return lax.rem(y + 4 + sign * dy, 4) * 2 + lax.rem(xh + lax.rem(b, 2), 2)

    def each(first, last, planes, sign, step):
        if first == 0:
            for a in range(7):
                step(a, planes[a] + across(0, sign))

        def body(b, carry):
            plane = across(b, sign)
            for a in range(8):
                step(b * 8 + a, planes[a] + plane)
            return carry

        lax.fori_loop(max(first, 1), last, body, 0)

    small = [
        pltpu.make_async_copy(a, b, small_sem.at[i])
        for i, (a, b) in enumerate(((q_hbm, qv), (nk_hbm, nkv), (nv_hbm, nvv)))
    ]
    for c in small:
        c.start()

    def kv_copies(g):
        rows = pl.ds(g * GROUP, GROUP)
        return (
            pltpu.make_async_copy(k_hbm.at[rows], kb.at[rows, pl.ds(0, CACHE)], kv_sem.at[0, g]),
            pltpu.make_async_copy(v_hbm.at[rows], vb.at[rows, pl.ds(0, CACHE)], kv_sem.at[1, g]),
        )

    for g in range(ROWS // GROUP):
        for c in kv_copies(g):
            c.start()
    weights = [
        pltpu.make_async_copy(
            wo_hbm.at[:, pl.ds(pl.multiple_of(block * 1024, 1024), 1024)], wo.at[i], w_sem.at[i]
        )
        for i, block in enumerate((near, near_far, far, t))
    ]
    weights.append(pltpu.make_async_copy(wd_hbm.at[0], wd, w_sem.at[4]))
    weights.append(pltpu.make_async_copy(wu_hbm.at[0], wu, w_sem.at[5]))
    barrier = pltpu.get_barrier_semaphore()

    def greet(k, d):
        pl.semaphore_signal(barrier, inc=1, device_id=(d, t), device_id_type=MESH)

    each(0, 8, ahead, 1, greet)
    for other in (near, far, near_far):
        pl.semaphore_signal(barrier, inc=1, device_id=(dp, other), device_id_type=MESH)

    for c in small:
        c.wait()
    for h in range(2):
        for s in range(2):
            for g in range(4):
                col = (h * 4 + g) * HEAD
                qs[h, pl.ds(s * 4 + g, ROWS, stride=8), :] = qv[s, :, col : col + HEAD].astype(jnp.float32)
    fresh[...] = jnp.zeros_like(fresh)
    for src, dst in ((nkv, kb), (nvv, vb)):
        for s in range(2):
            for h in range(2):
                fresh[h, pl.ds(s, ROWS, stride=16), :] = src[s, :, h * HEAD : (h + 1) * HEAD].astype(jnp.float32)
        for h in range(2):
            dst[:, CACHE:EXTENDED, h * HEAD : (h + 1) * HEAD] = (
                fresh[h].reshape(ROWS, 16, HEAD).astype(jnp.bfloat16)
            )

    ids = opp_ref[...]
    down = lax.broadcasted_iota(jnp.int32, (ROWS, ROWS), 0)
    along = lax.broadcasted_iota(jnp.int32, (ROWS, ROWS), 1)
    named = jnp.where(down == ids, 1.0, 0.0)
    before = jnp.where(down < along, 1.0, 0.0).astype(jnp.bfloat16)
    earlier = jnp.dot(named.astype(jnp.bfloat16), before, preferred_element_type=jnp.float32)
    rank = jnp.sum(named * earlier, axis=0, keepdims=True).astype(jnp.int32)
    slot = jnp.sum(jnp.where(down == along, 2 * ids + rank, 0), axis=1, keepdims=True)
    place_col[...] = jnp.broadcast_to(slot * 8, (ROWS, HEAD))
    lanes = lax.broadcasted_iota(jnp.int32, (ROWS, ROWS * 8), 1)
    rows_of = lax.broadcasted_iota(jnp.int32, (ROWS, ROWS * 8), 0)
    place_row[...] = jnp.sum(
        jnp.where((lanes >> 3) == rows_of, slot * 8 + (lanes & 7), 0), axis=0, keepdims=True
    )

    lane = lax.broadcasted_iota(jnp.int32, (8, EXTENDED), 1)
    sub = lax.broadcasted_iota(jnp.int32, (8, EXTENDED), 0)
    new_ok = (lane == CACHE) | ((lane == CACHE + 1) & (sub >= 4))
    zero = jnp.zeros((8, HEAD), jnp.float32)

    def probs(scores, r):
        ok = (lane < len_ref[r]) | new_ok
        scores = jnp.where(ok, scores * SCALE, -1e30)
        power = jnp.exp(scores - jnp.max(scores, axis=1, keepdims=True))
        return power / jnp.sum(power, axis=1, keepdims=True)

    def attend(g, carry):
        for c in kv_copies(g):
            c.wait()

        @pl.when(g == 2)
        def _():
            for c in weights:
                c.start()

        for j in range(4):
            first = g * 256 + j * 64
            at = lax.broadcasted_iota(jnp.int32, (64, ROWS * 8), 0) + first
            outward[pl.ds(pl.multiple_of(first, 64), 64), :] = jnp.where(
                at == place_row[...], 1.0, 0.0
            ).astype(jnp.bfloat16)
        rows = [g * GROUP + j for j in range(GROUP)]
        at = [pl.ds(pl.multiple_of(r * 8, 8), 8) for r in rows]
        scores = []
        for r, a in zip(rows, at):
            q = jnp.concatenate(
                [jnp.concatenate([qs[0, a, :], zero], 1), jnp.concatenate([zero, qs[1, a, :]], 1)], 0
            ).astype(jnp.bfloat16)
            scores.append(lax.dot_general(q, kb[r], CONTRACT_LAST, preferred_element_type=jnp.float32))
        ps = [
            jnp.concatenate([probs(s[:8], r), probs(s[8:], r)], 0).astype(jnp.bfloat16)
            for s, r in zip(scores, rows)
        ]
        both = []
        for p, r, a in zip(ps, rows, at):
            o = jnp.dot(p, vb[r], preferred_element_type=jnp.float32)
            att[0, a, :] = o[:8, :HEAD]
            att[1, a, :] = o[8:, HEAD:]
            both.append(jnp.concatenate([o[:8, :HEAD], o[8:, HEAD:]], 1))
        for i in range(GROUP // 2):
            pair = pl.ds(pl.multiple_of(g * GROUP * 8 + i * 16, 16), 16)
            attp[pair, :] = jnp.concatenate(both[2 * i : 2 * i + 2], 0).astype(jnp.bfloat16)
        return carry

    lax.fori_loop(0, ROWS // GROUP, attend, 0)

    pl.semaphore_wait(barrier, 66)

    def fill(i, carry):
        rows = pl.ds(pl.multiple_of(i * 256, 256), 256)
        filled = jnp.dot(outward[rows, :], attp[...], preferred_element_type=jnp.float32)
        send[pl.ds(pl.multiple_of(i * 16, 16), 16)] = filled.astype(jnp.bfloat16).reshape(16, 16, 256)
        return carry

    lax.fori_loop(0, 4, fill, 0)

    def dispatch(half):
        def step(k, d):
            pltpu.make_async_remote_copy(
                src_ref=send.at[d], dst_ref=recv.at[k], send_sem=d_send, recv_sem=d_recv.at[half],
                device_id=(d, t), device_id_type=MESH,
            ).start()

        each(4 * half, 4 * half + 4, ahead, 1, step)

    dispatch(0)
    recv[7] = send[dp]

    for h in range(2):
        for s in range(2):
            for g in range(4):
                col = (h * 4 + g) * HEAD
                attb[s * ROWS : (s + 1) * ROWS, col : col + HEAD] = att[
                    h, pl.ds(s * 4 + g, ROWS, stride=8), :
                ].astype(jnp.bfloat16)

    def base_block(i, store):
        weights[i].wait()

        def tile(n, carry):
            cols = pl.ds(pl.multiple_of(n * 256, 256), 256)
            store(cols, jnp.dot(attb[...], wo[i, :, cols], preferred_element_type=jnp.float32))
            return carry

        lax.fori_loop(0, 4, tile, 0)

    def remote(i, src, dst, other):
        return pltpu.make_async_remote_copy(
            src_ref=src, dst_ref=dst, send_sem=t_send.at[i], recv_sem=t_recv.at[i],
            device_id=(dp, other), device_id_type=MESH,
        )

    def send_near(i):
        def to_send(cols, value):
            bsend[i, :, cols] = value.astype(jnp.bfloat16)

        base_block(i, to_send)
        c = remote(i, bsend.at[i], brecv.at[i], near)
        c.start()
        return c

    def keep_block(i):
        def to_keep(cols, value):
            keep[i, :, cols] = value

        base_block(2 + i, to_keep)

    for_far = send_near(1)
    keep_block(0)
    for_far.wait()
    csend[...] = (keep[0] + brecv[1].astype(jnp.float32)).astype(jnp.bfloat16)
    base_far = [
        remote(2 + i, csend.at[pl.ds(i * ROWS, ROWS)], crecv.at[pl.ds(i * ROWS, ROWS)], far) for i in range(2)
    ]
    base_far[0].start()
    dispatch(1)
    base_near = send_near(0)
    keep_block(1)

    lane = lax.broadcasted_iota(jnp.int32, (ROWS, HEAD), 1)
    for c in range(4):
        for s in range(2):
            for n in range(8):
                homeward[(c * 2 + s) * ROWS : (c * 2 + s + 1) * ROWS, n * HEAD : (n + 1) * HEAD] = jnp.where(
                    lane + (n * HEAD - s * 4 - c) == place_col[...], 1.0, 0.0
                ).astype(jnp.bfloat16)

    weights[4].wait()
    weights[5].wait()

    def give_back(k, d):
        pltpu.make_async_remote_copy(
            src_ref=rsend.at[k], dst_ref=rrecv.at[dp], send_sem=r_send, recv_sem=r_recv,
            device_id=(d, t), device_id_type=MESH,
        ).start()

    for half in range(2):
        blocks = slice(half * 32, half * 32 + 32)
        count = 31 + half
        arrived = recv.at[pl.ds(half * 32, count)]
        pltpu.make_async_copy(arrived, arrived, d_recv.at[half]).wait()
        for h in range(2):
            recvf[h] = recv[blocks, :, h * HEAD : (h + 1) * HEAD].reshape(8 * ROWS, HEAD).astype(jnp.float32)
        received = jnp.concatenate(
            [
                recvf[h, pl.ds(g, 2 * ROWS, stride=4), :].astype(jnp.bfloat16)
                for h in range(2)
                for g in range(4)
            ],
            1,
        )
        part[half] = jnp.dot(received, wd[...], preferred_element_type=jnp.float32)
        c = remote(4 + half * 2, part.at[half], x1r.at[half], near)
        c.start()
        c.wait()
        pair[half] = (part[half] + x1r[half]).astype(jnp.bfloat16)
        c = remote(5 + half * 2, pair.at[half], x2r.at[half], far)
        c.start()
        c.wait()
        if half == 1:
            base_far[1].start()
        shrunk[half] = (part[half] + x1r[half] + x2r[half].astype(jnp.float32)).astype(jnp.bfloat16)
        for c in range(4):
            lifted = jnp.dot(shrunk[half], wu[:, c * 256 : (c + 1) * 256], preferred_element_type=jnp.float32)
            for h in range(2):
                liftf[h, pl.ds(c, 2 * ROWS, stride=4), :] = lifted[:, h * HEAD : (h + 1) * HEAD]
        for h in range(2):
            rsend[blocks, :, h * HEAD : (h + 1) * HEAD] = (
                liftf[h].reshape(ROWS // 2, 16, HEAD).astype(jnp.bfloat16)
            )
        if half == 0:
            rrecv[dp] = rsend[7]
        each(4 * half, 4 * half + 4, behind, -1, give_back)

    base_near.wait()
    for c in base_far:
        c.wait()
    keep[1] = keep[1] + brecv[0].astype(jnp.float32) + crecv[...].astype(jnp.float32)
    pltpu.make_async_copy(rrecv.at[pl.ds(0, 63)], rrecv.at[pl.ds(0, 63)], r_recv).wait()

    lifts = jnp.dot(homeward[...], rrecv[...].reshape(ROWS * 16, 256), preferred_element_type=jnp.float32)
    for c in range(4):
        for s in range(2):
            rows, first = slice(s * ROWS, (s + 1) * ROWS), (c * 2 + s) * ROWS
            cols = slice(c * 256, (c + 1) * 256)
            out_ref[s, :, cols] = (keep[1, rows, cols] + lifts[first : first + ROWS]).astype(jnp.bfloat16)
    pltpu.make_async_copy(send.at[pl.ds(0, 63)], send.at[pl.ds(0, 63)], d_send).wait()
    pltpu.make_async_copy(rsend.at[pl.ds(0, 63)], rsend.at[pl.ds(0, 63)], r_send).wait()


def local(
    queries,
    cached_key_rows,
    cached_value_rows,
    incoming_keys,
    incoming_values,
    output_weight,
    adapter_down_weight,
    adapter_up_weight,
    opponent,
    cache_length_rows,
):
    bf16, f32 = jnp.bfloat16, jnp.float32
    vmem, dma = pltpu.VMEM, pltpu.SemaphoreType.DMA
    hbm = pl.BlockSpec(memory_space=pl.ANY)
    smem = pl.BlockSpec(memory_space=pltpu.SMEM)
    return pl.pallas_call(
        kernel,
        out_shape=jax.ShapeDtypeStruct((2, ROWS, 1024), bf16),
        in_specs=[hbm] * 8 + [smem] + [pl.BlockSpec(memory_space=pltpu.VMEM)],
        out_specs=pl.BlockSpec(memory_space=pltpu.VMEM),
        scratch_shapes=[
            vmem((2, ROWS, 1024), bf16),
            vmem((2, ROWS, 256), bf16),
            vmem((2, ROWS, 256), bf16),
            vmem((ROWS, EXTENDED, 256), bf16),
            vmem((ROWS, EXTENDED, 256), bf16),
            vmem((2, ROWS * 16, HEAD), f32),
            vmem((2, ROWS * 8, HEAD), f32),
            vmem((2, ROWS * 8, HEAD), f32),
            vmem((ROWS * 8, 256), bf16),
            vmem((1, ROWS * 8), jnp.int32),
            vmem((ROWS, HEAD), jnp.int32),
            vmem((ROWS * 16, ROWS * 8), bf16),
            vmem((ROWS * 8, ROWS * 16), bf16),
            vmem((4, 1024, 1024), bf16),
            vmem((1024, 256), bf16),
            vmem((256, 1024), bf16),
            vmem((ROWS, 16, 256), bf16),
            vmem((ROWS, 16, 256), bf16),
            vmem((2, ROWS * 8, HEAD), f32),
            vmem((2, 128, 256), f32),
            vmem((2, 128, 256), f32),
            vmem((2, 128, 256), bf16),
            vmem((2, 128, 256), bf16),
            vmem((2, 128, 256), bf16),
            vmem((2, ROWS * 8, HEAD), f32),
            vmem((ROWS, 16, 256), bf16),
            vmem((ROWS, 16, 256), bf16),
            vmem((2 * ROWS, 1024), bf16),
            vmem((2, 2 * ROWS, 1024), bf16),
            vmem((2, 2 * ROWS, 1024), bf16),
            vmem((2, 2 * ROWS, 1024), f32),
            vmem((2 * ROWS, 1024), bf16),
            vmem((2 * ROWS, 1024), bf16),
            dma((3,)),
            dma((2, 4)),
            dma((6,)),
            dma,
            dma((2,)),
            dma,
            dma,
            dma((8,)),
            dma((8,)),
        ],
        compiler_params=pltpu.CompilerParams(
            collective_id=0, has_side_effects=True, vmem_limit_bytes=56 << 20
        ),
        cost_estimate=pl.CostEstimate(flops=1500000000, bytes_accessed=24000000, transcendentals=300000),
    )(
        queries,
        cached_key_rows,
        cached_value_rows,
        incoming_keys,
        incoming_values,
        output_weight,
        adapter_down_weight,
        adapter_up_weight,
        cache_length_rows,
        opponent.reshape(1, ROWS),
    )


def solution(mesh):
    in_specs = (
        P(None, "dp", "tensor"),
        P("dp", None, "tensor"),
        P("dp", None, "tensor"),
        P(None, "dp", "tensor"),
        P(None, "dp", "tensor"),
        P("tensor", None),
        P("dp", "tensor", None),
        P("dp", None, "tensor"),
        P("dp", None),
        P("dp"),
    )
    out_specs = P(None, "dp", "tensor")
    return jax.shard_map(local, mesh=mesh, in_specs=in_specs, out_specs=out_specs, check_vma=False)
```

```python
import math

import jax
import jax.numpy as jnp
from jax import lax
from jax.experimental import pallas as pl
from jax.experimental.pallas import tpu as pltpu
from jax.sharding import PartitionSpec as P

ROWS = 64
CACHE = 192
EXTENDED = 208
GROUP = 16
HEAD = 128
SCALE = 1.0 / math.sqrt(HEAD)
MESH = pl.DeviceIdType.MESH
CONTRACT_LAST = (((1,), (1,)), ((), ()))


def kernel(
    q_hbm, k_hbm, v_hbm, nk_hbm, nv_hbm, wo_hbm, wd_hbm, wu_hbm, len_ref, opp_ref,
    out_ref,
    qv, nkv, nvv, kb, vb, fresh, qs, att, attp, place_row, place_col, outward, homeward, wo, wd, wu,
    send, recv, recvf, part, x1r, pair, x2r, shrunk, liftf, rsend, rrecv,
    attb, bsend, brecv, keep, csend, crecv,
    small_sem, kv_sem, w_sem, d_send, d_recv, r_send, r_recv, t_send, t_recv,
):
    dp = lax.axis_index("dp")
    t = lax.axis_index("tensor")
    z, y, xh = dp // 8, lax.rem(dp // 2, 4), lax.rem(dp, 2)
    core = lax.rem(t, 2)
    near = t + 1 - 2 * core
    far = lax.rem(t + 2, 4)
    near_far = lax.rem(near + 2, 4)

    order = (4, 3, 5, 2, 6, 1, 7, 0)
    ahead = [lax.rem(z + dz, 8) * 8 for dz in order]
    behind = [lax.rem(z + 8 - dz, 8) * 8 for dz in order]

    def across(b, sign):
        c = b // 2
        dy = lax.rem(2 * c, 4) + c // 2
        return lax.rem(y + 4 + sign * dy, 4) * 2 + lax.rem(xh + lax.rem(b, 2), 2)

    def each(first, last, planes, sign, step):
        if first == 0:
            for a in range(7):
                step(a, planes[a] + across(0, sign))

        def body(b, carry):
            plane = across(b, sign)
            for a in range(8):
                step(b * 8 + a, planes[a] + plane)
            return carry

        lax.fori_loop(max(first, 1), last, body, 0)

    small = [
        pltpu.make_async_copy(a, b, small_sem.at[i])
        for i, (a, b) in enumerate(((q_hbm, qv), (nk_hbm, nkv), (nv_hbm, nvv)))
    ]
    for c in small:
        c.start()

    def kv_copies(g):
        rows = pl.ds(g * GROUP, GROUP)
        return (
            pltpu.make_async_copy(k_hbm.at[rows], kb.at[rows, pl.ds(0, CACHE)], kv_sem.at[0, g]),
            pltpu.make_async_copy(v_hbm.at[rows], vb.at[rows, pl.ds(0, CACHE)], kv_sem.at[1, g]),
        )

    for g in range(ROWS // GROUP):
        for c in kv_copies(g):
            c.start()
    weights = [
        pltpu.make_async_copy(
            wo_hbm.at[:, pl.ds(pl.multiple_of(block * 1024, 1024), 1024)], wo.at[i], w_sem.at[i]
        )
        for i, block in enumerate((near, near_far, far, t))
    ]
    weights.append(pltpu.make_async_copy(wd_hbm.at[0], wd, w_sem.at[4]))
    weights.append(pltpu.make_async_copy(wu_hbm.at[0], wu, w_sem.at[5]))
    barrier = pltpu.get_barrier_semaphore()

    def greet(k, d):
        pl.semaphore_signal(barrier, inc=1, device_id=(d, t), device_id_type=MESH)

    each(0, 8, ahead, 1, greet)
    for other in (near, far, near_far):
        pl.semaphore_signal(barrier, inc=1, device_id=(dp, other), device_id_type=MESH)

    for c in small:
        c.wait()
    for h in range(2):
        for s in range(2):
            for g in range(4):
                col = (h * 4 + g) * HEAD
                qs[h, pl.ds(s * 4 + g, ROWS, stride=8), :] = qv[s, :, col : col + HEAD].astype(jnp.float32)
    fresh[...] = jnp.zeros_like(fresh)
    for src, dst in ((nkv, kb), (nvv, vb)):
        for s in range(2):
            for h in range(2):
                fresh[h, pl.ds(s, ROWS, stride=16), :] = src[s, :, h * HEAD : (h + 1) * HEAD].astype(jnp.float32)
        for h in range(2):
            dst[:, CACHE:EXTENDED, h * HEAD : (h + 1) * HEAD] = (
                fresh[h].reshape(ROWS, 16, HEAD).astype(jnp.bfloat16)
            )

    ids = opp_ref[...]
    down = lax.broadcasted_iota(jnp.int32, (ROWS, ROWS), 0)
    along = lax.broadcasted_iota(jnp.int32, (ROWS, ROWS), 1)
    named = jnp.where(down == ids, 1.0, 0.0)
    before = jnp.where(down < along, 1.0, 0.0).astype(jnp.bfloat16)
    earlier = jnp.dot(named.astype(jnp.bfloat16), before, preferred_element_type=jnp.float32)
    rank = jnp.sum(named * earlier, axis=0, keepdims=True).astype(jnp.int32)
    slot = jnp.sum(jnp.where(down == along, 2 * ids + rank, 0), axis=1, keepdims=True)
    place_col[...] = jnp.broadcast_to(slot * 8, (ROWS, HEAD))
    lanes = lax.broadcasted_iota(jnp.int32, (ROWS, ROWS * 8), 1)
    rows_of = lax.broadcasted_iota(jnp.int32, (ROWS, ROWS * 8), 0)
    place_row[...] = jnp.sum(
        jnp.where((lanes >> 3) == rows_of, slot * 8 + (lanes & 7), 0), axis=0, keepdims=True
    )

    lane = lax.broadcasted_iota(jnp.int32, (8, EXTENDED), 1)
    sub = lax.broadcasted_iota(jnp.int32, (8, EXTENDED), 0)
    new_ok = (lane == CACHE) | ((lane == CACHE + 1) & (sub >= 4))
    zero = jnp.zeros((8, HEAD), jnp.float32)

    def probs(scores, r):
        ok = (lane < len_ref[r]) | new_ok
        scores = jnp.where(ok, scores * SCALE, -1e30)
        power = jnp.exp(scores - jnp.max(scores, axis=1, keepdims=True))
        return power / jnp.sum(power, axis=1, keepdims=True)

    def attend(g, carry):
        for c in kv_copies(g):
            c.wait()

        @pl.when(g == 3)
        def _():
            for c in weights:
                c.start()

        for j in range(4):
            first = g * 256 + j * 64
            at = lax.broadcasted_iota(jnp.int32, (64, ROWS * 8), 0) + first
            outward[pl.ds(pl.multiple_of(first, 64), 64), :] = jnp.where(
                at == place_row[...], 1.0, 0.0
            ).astype(jnp.bfloat16)
        rows = [g * GROUP + j for j in range(GROUP)]
        at = [pl.ds(pl.multiple_of(r * 8, 8), 8) for r in rows]
        scores = []
        for r, a in zip(rows, at):
            q = jnp.concatenate(
                [jnp.concatenate([qs[0, a, :], zero], 1), jnp.concatenate([zero, qs[1, a, :]], 1)], 0
            ).astype(jnp.bfloat16)
            scores.append(lax.dot_general(q, kb[r], CONTRACT_LAST, preferred_element_type=jnp.float32))
        ps = [
            jnp.concatenate([probs(s[:8], r), probs(s[8:], r)], 0).astype(jnp.bfloat16)
            for s, r in zip(scores, rows)
        ]
        both = []
        for p, r, a in zip(ps, rows, at):
            o = jnp.dot(p, vb[r], preferred_element_type=jnp.float32)
            att[0, a, :] = o[:8, :HEAD]
            att[1, a, :] = o[8:, HEAD:]
            both.append(jnp.concatenate([o[:8, :HEAD], o[8:, HEAD:]], 1))
        for i in range(GROUP // 2):
            pair = pl.ds(pl.multiple_of(g * GROUP * 8 + i * 16, 16), 16)
            attp[pair, :] = jnp.concatenate(both[2 * i : 2 * i + 2], 0).astype(jnp.bfloat16)
        return carry

    lax.fori_loop(0, ROWS // GROUP, attend, 0)

    pl.semaphore_wait(barrier, 66)

    def fill(i, carry):
        rows = pl.ds(pl.multiple_of(i * 256, 256), 256)
        filled = jnp.dot(outward[rows, :], attp[...], preferred_element_type=jnp.float32)
        send[pl.ds(pl.multiple_of(i * 16, 16), 16)] = filled.astype(jnp.bfloat16).reshape(16, 16, 256)
        return carry

    lax.fori_loop(0, 4, fill, 0)

    def dispatch(half):
        def step(k, d):
            pltpu.make_async_remote_copy(
                src_ref=send.at[d], dst_ref=recv.at[k], send_sem=d_send, recv_sem=d_recv.at[half],
                device_id=(d, t), device_id_type=MESH,
            ).start()

        each(4 * half, 4 * half + 4, ahead, 1, step)

    dispatch(0)
    recv[7] = send[dp]

    for h in range(2):
        for s in range(2):
            for g in range(4):
                col = (h * 4 + g) * HEAD
                attb[s * ROWS : (s + 1) * ROWS, col : col + HEAD] = att[
                    h, pl.ds(s * 4 + g, ROWS, stride=8), :
                ].astype(jnp.bfloat16)

    def base_block(i, store):
        weights[i].wait()

        def tile(n, carry):
            cols = pl.ds(pl.multiple_of(n * 256, 256), 256)
            store(cols, jnp.dot(attb[...], wo[i, :, cols], preferred_element_type=jnp.float32))
            return carry

        lax.fori_loop(0, 4, tile, 0)

    def remote(i, src, dst, other):
        return pltpu.make_async_remote_copy(
            src_ref=src, dst_ref=dst, send_sem=t_send.at[i], recv_sem=t_recv.at[i],
            device_id=(dp, other), device_id_type=MESH,
        )

    def send_near(i):
        def to_send(cols, value):
            bsend[i, :, cols] = value.astype(jnp.bfloat16)

        base_block(i, to_send)
        c = remote(i, bsend.at[i], brecv.at[i], near)
        c.start()
        return c

    def keep_block(i):
        def to_keep(cols, value):
            keep[i, :, cols] = value

        base_block(2 + i, to_keep)

    for_far = send_near(1)
    keep_block(0)
    for_far.wait()
    csend[...] = (keep[0] + brecv[1].astype(jnp.float32)).astype(jnp.bfloat16)
    base_far = [
        remote(2 + i, csend.at[pl.ds(i * ROWS, ROWS)], crecv.at[pl.ds(i * ROWS, ROWS)], far) for i in range(2)
    ]
    base_far[0].start()
    dispatch(1)
    base_near = send_near(0)
    keep_block(1)

    lane = lax.broadcasted_iota(jnp.int32, (ROWS, HEAD), 1)
    for c in range(4):
        for s in range(2):
            for n in range(8):
                homeward[(c * 2 + s) * ROWS : (c * 2 + s + 1) * ROWS, n * HEAD : (n + 1) * HEAD] = jnp.where(
                    lane + (n * HEAD - s * 4 - c) == place_col[...], 1.0, 0.0
                ).astype(jnp.bfloat16)

    weights[4].wait()
    weights[5].wait()

    def give_back(k, d):
        pltpu.make_async_remote_copy(
            src_ref=rsend.at[k], dst_ref=rrecv.at[dp], send_sem=r_send, recv_sem=r_recv,
            device_id=(d, t), device_id_type=MESH,
        ).start()

    for half in range(2):
        blocks = slice(half * 32, half * 32 + 32)
        count = 31 + half
        arrived = recv.at[pl.ds(half * 32, count)]
        pltpu.make_async_copy(arrived, arrived, d_recv.at[half]).wait()
        for h in range(2):
            recvf[h] = recv[blocks, :, h * HEAD : (h + 1) * HEAD].reshape(8 * ROWS, HEAD).astype(jnp.float32)
        received = jnp.concatenate(
            [
                recvf[h, pl.ds(g, 2 * ROWS, stride=4), :].astype(jnp.bfloat16)
                for h in range(2)
                for g in range(4)
            ],
            1,
        )
        part[half] = jnp.dot(received, wd[...], preferred_element_type=jnp.float32)
        c = remote(4 + half * 2, part.at[half], x1r.at[half], near)
        c.start()
        c.wait()
        pair[half] = (part[half] + x1r[half]).astype(jnp.bfloat16)
        c = remote(5 + half * 2, pair.at[half], x2r.at[half], far)
        c.start()
        c.wait()
        if half == 1:
            base_far[1].start()
        shrunk[half] = (part[half] + x1r[half] + x2r[half].astype(jnp.float32)).astype(jnp.bfloat16)
        for c in range(4):
            lifted = jnp.dot(shrunk[half], wu[:, c * 256 : (c + 1) * 256], preferred_element_type=jnp.float32)
            for h in range(2):
                liftf[h, pl.ds(c, 2 * ROWS, stride=4), :] = lifted[:, h * HEAD : (h + 1) * HEAD]
        for h in range(2):
            rsend[blocks, :, h * HEAD : (h + 1) * HEAD] = (
                liftf[h].reshape(ROWS // 2, 16, HEAD).astype(jnp.bfloat16)
            )
        if half == 0:
            rrecv[dp] = rsend[7]
        each(4 * half, 4 * half + 4, behind, -1, give_back)

    base_near.wait()
    for c in base_far:
        c.wait()
    keep[1] = keep[1] + brecv[0].astype(jnp.float32) + crecv[...].astype(jnp.float32)
    pltpu.make_async_copy(rrecv.at[pl.ds(0, 63)], rrecv.at[pl.ds(0, 63)], r_recv).wait()

    lifts = jnp.dot(homeward[...], rrecv[...].reshape(ROWS * 16, 256), preferred_element_type=jnp.float32)
    for c in range(4):
        for s in range(2):
            rows, first = slice(s * ROWS, (s + 1) * ROWS), (c * 2 + s) * ROWS
            cols = slice(c * 256, (c + 1) * 256)
            out_ref[s, :, cols] = (keep[1, rows, cols] + lifts[first : first + ROWS]).astype(jnp.bfloat16)
    pltpu.make_async_copy(send.at[pl.ds(0, 63)], send.at[pl.ds(0, 63)], d_send).wait()
    pltpu.make_async_copy(rsend.at[pl.ds(0, 63)], rsend.at[pl.ds(0, 63)], r_send).wait()


def local(
    queries,
    cached_key_rows,
    cached_value_rows,
    incoming_keys,
    incoming_values,
    output_weight,
    adapter_down_weight,
    adapter_up_weight,
    opponent,
    cache_length_rows,
):
    bf16, f32 = jnp.bfloat16, jnp.float32
    vmem, dma = pltpu.VMEM, pltpu.SemaphoreType.DMA
    hbm = pl.BlockSpec(memory_space=pl.ANY)
    smem = pl.BlockSpec(memory_space=pltpu.SMEM)
    return pl.pallas_call(
        kernel,
        out_shape=jax.ShapeDtypeStruct((2, ROWS, 1024), bf16),
        in_specs=[hbm] * 8 + [smem] + [pl.BlockSpec(memory_space=pltpu.VMEM)],
        out_specs=pl.BlockSpec(memory_space=pltpu.VMEM),
        scratch_shapes=[
            vmem((2, ROWS, 1024), bf16),
            vmem((2, ROWS, 256), bf16),
            vmem((2, ROWS, 256), bf16),
            vmem((ROWS, EXTENDED, 256), bf16),
            vmem((ROWS, EXTENDED, 256), bf16),
            vmem((2, ROWS * 16, HEAD), f32),
            vmem((2, ROWS * 8, HEAD), f32),
            vmem((2, ROWS * 8, HEAD), f32),
            vmem((ROWS * 8, 256), bf16),
            vmem((1, ROWS * 8), jnp.int32),
            vmem((ROWS, HEAD), jnp.int32),
            vmem((ROWS * 16, ROWS * 8), bf16),
            vmem((ROWS * 8, ROWS * 16), bf16),
            vmem((4, 1024, 1024), bf16),
            vmem((1024, 256), bf16),
            vmem((256, 1024), bf16),
            vmem((ROWS, 16, 256), bf16),
            vmem((ROWS, 16, 256), bf16),
            vmem((2, ROWS * 8, HEAD), f32),
            vmem((2, 128, 256), f32),
            vmem((2, 128, 256), f32),
            vmem((2, 128, 256), bf16),
            vmem((2, 128, 256), bf16),
            vmem((2, 128, 256), bf16),
            vmem((2, ROWS * 8, HEAD), f32),
            vmem((ROWS, 16, 256), bf16),
            vmem((ROWS, 16, 256), bf16),
            vmem((2 * ROWS, 1024), bf16),
            vmem((2, 2 * ROWS, 1024), bf16),
            vmem((2, 2 * ROWS, 1024), bf16),
            vmem((2, 2 * ROWS, 1024), f32),
            vmem((2 * ROWS, 1024), bf16),
            vmem((2 * ROWS, 1024), bf16),
            dma((3,)),
            dma((2, 4)),
            dma((6,)),
            dma,
            dma((2,)),
            dma,
            dma,
            dma((8,)),
            dma((8,)),
        ],
        compiler_params=pltpu.CompilerParams(
            collective_id=0, has_side_effects=True, vmem_limit_bytes=56 << 20
        ),
        cost_estimate=pl.CostEstimate(flops=1500000000, bytes_accessed=24000000, transcendentals=300000),
    )(
        queries,
        cached_key_rows,
        cached_value_rows,
        incoming_keys,
        incoming_values,
        output_weight,
        adapter_down_weight,
        adapter_up_weight,
        cache_length_rows,
        opponent.reshape(1, ROWS),
    )


def solution(mesh):
    in_specs = (
        P(None, "dp", "tensor"),
        P("dp", None, "tensor"),
        P("dp", None, "tensor"),
        P(None, "dp", "tensor"),
        P(None, "dp", "tensor"),
        P("tensor", None),
        P("dp", "tensor", None),
        P("dp", None, "tensor"),
        P("dp", None),
        P("dp"),
    )
    out_specs = P(None, "dp", "tensor")
    return jax.shard_map(local, mesh=mesh, in_specs=in_specs, out_specs=out_specs, check_vma=False)
```
